256 devices in a mesh: band: 8 (over z_hi, core), plane: 32 (over x, y, z_lo).
Axes of the slice: x: 4, y: 4, z: 8 (z_hi: 4, z_lo: 2; z = z_hi * 2 + z_lo), core: 2. Of those that a mesh axis runs over, the one named last changes fastest.
Arguments:
- targets: float32 [16, 128, 128, 128], P('band', 'plane'), may hold values from -6 to 6
- sources: float32 [8, 128, 128, 128], P('band', 'plane'), may hold values from -6 to 6
- kernel: float32 [128, 128, 128], P(None, 'plane'), as said below
Outputs:
- fock_applied: float32 [16, 128, 128, 128], P('band', 'plane')
The draws below stay inside these ranges and needn't reach their ends.
Inputs may be any that keep to these rules, and one draw needn't show every extreme that they name: kernel is positive and even: kernel[a, b, c] equals kernel[(-a) mod 128, (-b) mod 128, (-c) mod 128].
All inputs are finite; a program needn't handle non-finite values.
Results may differ from the reference program's by a relative error of at most 0.0001.
Values sent between devices are 32-bit elements; how exact they have to be, the bound alone decides.
No kernel may reach another device: no remote copies, remote signals or barrier semaphores. Data moves between devices by JAX's collectives and lax.ppermute only.
A program may use at most 64 MiB of HBM per device.

```python
import math
import jax
import jax.numpy as jnp
from jax import lax

GRID = 128
TARGETS = 16
SOURCES = 8


def draw_kernel(key, part):
    key = jax.random.fold_in(key, 7)
    screening = 0.25
    log_spread = math.log(2.0)
    indices = jnp.arange(GRID, dtype=jnp.int32)
    frequency = jnp.where(indices < GRID // 2, indices, indices - GRID).astype(jnp.float32)
    squared = frequency[:, None, None] ** 2 + frequency[None, :, None] ** 2 + frequency[None, None, :] ** 2
    coulomb = 2.0 / (1.0 + squared / (screening * GRID) ** 2)
    roughness = jax.random.uniform(key, (GRID, GRID, GRID), jnp.float32, -log_spread, log_spread)
    mirror = roughness
    for dimension in range(3):
        mirror = jnp.roll(jnp.flip(mirror, dimension), 1, dimension)
    return coulomb * jnp.exp(0.5 * (roughness + mirror))


def block_levels(key, shape, cuts, smallest, top_value):
    def one(axis_at, shards_of):
        steps = jax.random.uniform(jax.random.fold_in(jax.random.fold_in(key, 6), axis_at), (shards_of,), jnp.float32, smallest / len(cuts), top_value / len(cuts))
        return jnp.repeat(jnp.exp(steps), shape[axis_at] // shards_of).reshape((-1,) + (1,) * (len(shape) - axis_at - 1))

    gain = one(*cuts[0])
    for cut in cuts[1:]:
        gain = gain * one(*cut)
    return gain


def gaussian(key, shape, scale, most, pieces=(), kind=jnp.bfloat16):
    array = scale * jax.random.normal(key, shape, jnp.float32)
    if pieces:
        array = array * block_levels(key, shape, pieces, -0.22, 0.18)
    return jnp.clip(array, -most, most).astype(kind)


def setup_inputs(seed: int = 0) -> dict:
    streams_of = jax.random.split(jax.random.key(seed), 4)
    return {
        "targets": gaussian(streams_of[0], (TARGETS, GRID, GRID, GRID), 1.0, 6.0, ((0, 8), (1, 32)), jnp.float32),
        "sources": gaussian(streams_of[1], (SOURCES, GRID, GRID, GRID), 1.0, 6.0, ((0, 8), (1, 32)), jnp.float32),
        "kernel": draw_kernel(jax.random.fold_in(streams_of[3], 71), 0),
    }


exact_share = 0.25


def reference(targets, sources, kernel):
    def single_band(target):
        def add_source(summed, source):
            density = source * target
            potential = jnp.real(jnp.fft.ifftn(kernel * jnp.fft.fftn(density)))
            return summed + potential * source, None

        summed, _ = lax.scan(add_source, jnp.zeros_like(target), sources)
        return -exact_share * summed

    return lax.map(single_band, targets)
```

```python
import math

import jax
import jax.numpy as jnp
import ml_dtypes
import numpy as np
from jax import lax
from jax.experimental import pallas as pl
from jax.experimental.pallas import tpu as pltpu
from jax.sharding import PartitionSpec as P

exact_share = 0.25
vmem_limit = 48 * 1024 * 1024


def halves(matrix):
    high = matrix.astype(ml_dtypes.bfloat16)
    low = (matrix - high.astype(np.float64)).astype(ml_dtypes.bfloat16)
    return np.stack([high, low])


def dft_matrices(length, planes):
    indices = np.arange(length)
    angles = (indices[:, None] * indices[None, :] % length) * (2.0 * math.pi / length)
    cosine, sine = np.cos(angles), np.sin(angles)
    forward = np.block([[cosine, sine], [-sine, cosine]])
    inverse = np.block([[cosine, -sine], [sine, cosine]])
    order = np.arange(2 * length).reshape(2, length // planes, planes).transpose(1, 0, 2).reshape(-1)
    return (
        halves(forward.T),
        halves(forward),
        halves(forward[:, order]),
        halves(inverse[order, :]),
        halves(inverse),
        halves(inverse.T),
    )


def split(values):
    high = values.astype(jnp.bfloat16)
    low = (values - high.astype(jnp.float32)).astype(jnp.bfloat16)
    return high, low


def dot(left, right):
    return jnp.dot(left, right, preferred_element_type=jnp.float32)


def from_left(matrix_ref, values):
    high, low = split(values)
    return dot(matrix_ref[0], high) + dot(matrix_ref[0], low) + dot(matrix_ref[1], high)


def from_right(values, matrix_ref):
    high, low = split(values)
    return dot(high, matrix_ref[0]) + dot(low, matrix_ref[0]) + dot(high, matrix_ref[1])


def forward_kernel(length, planes, targets_ref, source_ref, z_ref, y_ref, out_ref):
    rows = planes * length
    source = source_ref[...].reshape(rows, length)
    density = jnp.concatenate(
        [targets_ref[part].reshape(rows, length) * source for part in range(2)], axis=1
    )
    along_z = from_right(density, z_ref)
    stacked = jnp.concatenate(
        [
            jnp.concatenate(
                [
                    along_z[p * length : (p + 1) * length, part * length : (part + 1) * length]
                    for part in range(2)
                ],
                axis=0,
            )
            for p in range(planes)
        ],
        axis=1,
    )
    along_y = from_left(y_ref, stacked)
    flat = out_ref.reshape(length * 2 * planes, length)
    for part in range(2):
        for p in range(planes):
            flat[pl.ds(part * planes + p, length, stride=2 * planes), :] = along_y[
                part * length : (part + 1) * length, p * length : (p + 1) * length
            ]


def middle_kernel(length, planes, values_ref, kernel_ref, x_ref, back_ref, out_ref):
    group = 2 * planes
    parts = length // planes
    values = jnp.concatenate(
        [
            values_ref[:, k * group : (k + 1) * group, :].reshape(2 * length, length)
            for k in range(planes)
        ],
        axis=1,
    )
    spectrum = from_left(x_ref, values)
    weight = jnp.concatenate([kernel_ref[k] for k in range(planes)], axis=1)
    weighted = jnp.concatenate([spectrum[:length] * weight, spectrum[length:] * weight], axis=0)
    back = from_left(back_ref, weighted)
    for k in range(planes):
        out_ref[:, k * group : (k + 1) * group, :] = back[
            :, k * length : (k + 1) * length
        ].reshape(parts, group, length)


def backward_kernel(length, planes, scale, values_ref, source_ref, y_ref, z_ref, sum_ref, out_ref):
    rows = planes * length
    flat = values_ref.reshape(length * 2 * planes, length)
    stacked = jnp.concatenate(
        [
            jnp.concatenate(
                [flat[pl.ds(part * planes + p, length, stride=2 * planes), :] for p in range(planes)],
                axis=1,
            )
            for part in range(2)
        ],
        axis=0,
    )
    along_y = from_left(y_ref, stacked)
    unstacked = jnp.concatenate(
        [
            jnp.concatenate(
                [
                    along_y[part * length : (part + 1) * length, p * length : (p + 1) * length]
                    for part in range(2)
                ],
                axis=1,
            )
            for p in range(planes)
        ],
        axis=0,
    )
    potential = from_right(unstacked, z_ref)
    source = source_ref[...].reshape(rows, length) * scale

    @pl.when(pl.program_id(0) == 0)
    def _():
        out_ref[...] = sum_ref[...]

    for part in range(2):
        term = potential[:, part * length : (part + 1) * length] * source
        out_ref[part] += term.reshape(planes, length, length)


def whole(shape):
    return pl.BlockSpec(shape, lambda s: (0,) * len(shape))


def params():
    return pltpu.CompilerParams(vmem_limit_bytes=vmem_limit, dimension_semantics=("arbitrary",))


def cost(count, rows, columns, passes):
    return pl.CostEstimate(
        flops=count * passes * 6 * rows * rows * columns,
        bytes_accessed=count * 3 * 4 * rows * columns,
        transcendentals=0,
    )


def solution(mesh):
    shards = mesh.shape["plane"]

    def on_device(targets, sources, kernel):
        length = targets.shape[-1]
        planes = targets.shape[1]
        group = 2 * planes * planes
        z_fwd, y_fwd, x_fwd, x_bwd, y_bwd, z_bwd = (
            jnp.asarray(m) for m in dft_matrices(length, planes)
        )
        square = (2, 2 * length, 2 * length)
        slab = pl.BlockSpec((None, planes, length, length), lambda s: (s, 0, 0, 0))
        block = pl.BlockSpec((shards, None, group, length), lambda s: (0, s, 0, 0))
        fields = (2, planes, length, length)
        grid_kernel = (kernel * (1.0 / float(length) ** 3)).transpose(1, 0, 2)

        def packed(count):
            return jax.ShapeDtypeStruct((shards, count, group, length), jnp.float32)

        def exchange(values):
            return lax.all_to_all(values, "plane", split_axis=0, concat_axis=0, tiled=True)

        def forward(batch):
            count = batch.shape[0]
            return pl.pallas_call(
                lambda *refs: forward_kernel(length, planes, *refs),
                grid=(count,),
                in_specs=[whole(fields), slab, whole(square), whole(square)],
                out_specs=block,
                out_shape=packed(count),
                compiler_params=params(),
                cost_estimate=cost(count, 2 * length, planes * length, 2),
                name="forward",
            )(targets, batch, z_fwd, y_fwd)

        def middle(values):
            count = values.shape[1]
            return pl.pallas_call(
                lambda *refs: middle_kernel(length, planes, *refs),
                grid=(count,),
                in_specs=[block, whole((planes, length, length)), whole(square), whole(square)],
                out_specs=block,
                out_shape=packed(count),
                compiler_params=params(),
                cost_estimate=cost(count, 2 * length, planes * length, 2),
                name="middle",
            )(values, grid_kernel, x_fwd, x_bwd)

        def backward(values, batch, summed):
            count = values.shape[1]
            return pl.pallas_call(
                lambda *refs: backward_kernel(length, planes, -exact_share, *refs),
                grid=(count,),
                in_specs=[block, slab, whole(square), whole(square), whole(fields)],
                out_specs=whole(fields),
                out_shape=jax.ShapeDtypeStruct(fields, jnp.float32),
                compiler_params=params(),
                cost_estimate=cost(count, 2 * length, planes * length, 2),
                name="backward",
            )(values, batch, y_bwd, z_bwd, summed)

        everyone = lax.all_gather(sources, "band", axis=0, tiled=True)
        half = everyone.shape[0] // 2
        batches = [everyone[:half], everyone[half:]]
        there = [exchange(forward(batch)) for batch in batches]
        here = [exchange(middle(values)) for values in there]
        summed = jnp.zeros_like(targets)
        for values, batch in zip(here, batches):
            summed = backward(values, batch, summed)
        return summed

    return jax.shard_map(
        on_device,
        mesh=mesh,
        in_specs=(
            P("band", "plane", None, None),
            P("band", "plane", None, None),
            P(None, "plane", None),
        ),
        out_specs=P("band", "plane", None, None),
        check_vma=False,
    )
```

```python
import math

import jax
import jax.numpy as jnp
import ml_dtypes
import numpy as np
from jax import lax
from jax.experimental import pallas as pl
from jax.experimental.pallas import tpu as pltpu
from jax.sharding import PartitionSpec as P

exact_share = 0.25
vmem_limit = 64 * 1024 * 1024


def halves(matrix):
    high = matrix.astype(ml_dtypes.bfloat16)
    low = (matrix - high.astype(np.float64)).astype(ml_dtypes.bfloat16)
    return high, low


def left_form(matrix):
    high, low = halves(matrix)
    return np.concatenate([high, high, low], axis=1)


def right_form(matrix):
    high, low = halves(matrix)
    return np.concatenate([high, high, low], axis=0)


def dft_matrices(length, planes):
    indices = np.arange(length)
    angles = (indices[:, None] * indices[None, :] % length) * (2.0 * math.pi / length)
    cosine, sine = np.cos(angles), np.sin(angles)
    forward = np.block([[cosine, sine], [-sine, cosine]])
    inverse = np.block([[cosine, -sine], [sine, cosine]])
    order = np.arange(2 * length).reshape(2, length // planes, planes).transpose(1, 0, 2).reshape(-1)
    return (
        (right_form(forward.T), left_form(forward)),
        (left_form(forward[:, order]), left_form(inverse[order, :])),
        (left_form(inverse), right_form(inverse.T)),
    )


def split(values):
    high = values.astype(jnp.bfloat16)
    low = (values - high.astype(jnp.float32)).astype(jnp.bfloat16)
    return high, low


def from_left(matrix_ref, values):
    high, low = split(values)
    stack = jnp.concatenate([high, low, high], axis=0)
    return jnp.dot(matrix_ref[...], stack, preferred_element_type=jnp.float32)


def from_right(values, matrix_ref):
    high, low = split(values)
    stack = jnp.concatenate([high, low, high], axis=1)
    return jnp.dot(stack, matrix_ref[...], preferred_element_type=jnp.float32)


def fetch(pairs, sems):
    copies = [
        pltpu.make_async_copy(source, target, sems.at[i]) for i, (source, target) in enumerate(pairs)
    ]
    for copy in copies:
        copy.start()
    return copies


def turn(values, length, count):
    return jnp.concatenate(
        [
            jnp.concatenate(
                [
                    values[p * length : (p + 1) * length, part * length : (part + 1) * length]
                    for part in range(2)
                ],
                axis=0,
            )
            for p in range(count)
        ],
        axis=1,
    )


def turn_back(values, length, count):
    return jnp.concatenate(
        [
            jnp.concatenate(
                [
                    values[part * length : (part + 1) * length, p * length : (p + 1) * length]
                    for part in range(2)
                ],
                axis=1,
            )
            for p in range(count)
        ],
        axis=0,
    )


def forward_kernel(length, planes, count, bounds_ref, targets_hbm, z_hbm, y_hbm, *refs):
    sources_hbm = refs[:count]
    out_hbm, targets_ref, z_ref, y_ref, sources_ref, out_ref, in_sems, source_sems, out_sems = refs[-9:]
    low, high = bounds_ref[0], bounds_ref[1]
    rows = planes * length
    items = 2 * planes

    def source_copy(i):
        return pltpu.make_async_copy(sources_hbm[i].at[0], sources_ref.at[i], source_sems.at[i])

    def out_copy(i):
        return pltpu.make_async_copy(out_ref.at[i], out_hbm.at[:, i], out_sems.at[i])

    @pl.when(low < high)
    def _():
        fixed = fetch([(targets_hbm, targets_ref), (z_hbm, z_ref), (y_hbm, y_ref)], in_sems)
        for i in range(count):

            @pl.when((low <= i) & (i < high))
            def _(i=i):
                source_copy(i).start()

        for copy in fixed:
            copy.wait()

        def step(n, carry):
            these = [2 * n, 2 * n + 1]
            for i in these:
                pltpu.make_async_copy(
                    sources_hbm[0].at[0], sources_ref.at[i], source_sems.at[i]
                ).wait()
            density = jnp.concatenate(
                [
                    jnp.concatenate(
                        [
                            (targets_ref[part] * sources_ref[i]).reshape(rows, length)
                            for part in range(2)
                        ],
                        axis=1,
                    )
                    for i in these
                ],
                axis=0,
            )
            along_y = from_left(y_ref, turn(from_right(density, z_ref), length, items))
            for at, i in enumerate(these):
                flat = out_ref.at[i].reshape(length * 2 * planes, length)
                for part in range(2):
                    for p in range(planes):
                        item = at * planes + p
                        flat[pl.ds(part * planes + p, length, stride=2 * planes), :] = along_y[
                            part * length : (part + 1) * length, item * length : (item + 1) * length
                        ]
                out_copy(i).start()
            return carry

        lax.fori_loop(low // 2, high // 2, step, 0)
        for i in range(count):

            @pl.when((low <= i) & (i < high))
            def _(i=i):
                out_copy(i).wait()


def middle_kernel(length, planes, count, *refs):
    values_hbm, kernel_hbm, there_hbm, back_hbm, out_hbm = refs[:5]
    values_ref, kernel_ref, there_ref, back_ref, out_ref, in_sems, value_sems, out_sems = refs[5:]
    group = 2 * planes
    parts = length // planes
    fixed = fetch(
        [(kernel_hbm, kernel_ref), (there_hbm, there_ref), (back_hbm, back_ref)], in_sems
    )
    fetch([(values_hbm.at[:, i], values_ref.at[i]) for i in range(count)], value_sems)
    for copy in fixed:
        copy.wait()

    def out_copy(i):
        return pltpu.make_async_copy(out_ref.at[i], out_hbm.at[:, i], out_sems.at[i])

    def step(n, carry):
        these = [2 * n, 2 * n + 1]
        for i in these:
            pltpu.make_async_copy(values_hbm.at[:, i], values_ref.at[i], value_sems.at[i]).wait()
        items = [(i, k) for i in these for k in range(planes)]
        values = jnp.concatenate(
            [
                values_ref[i, :, k * group : (k + 1) * group, :].reshape(2 * length, length)
                for i, k in items
            ],
            axis=1,
        )
        spectrum = from_left(there_ref, values)
        weight = jnp.concatenate([kernel_ref[k] for i, k in items], axis=1)
        weighted = jnp.concatenate([spectrum[:length] * weight, spectrum[length:] * weight], axis=0)
        back = from_left(back_ref, weighted)
        for at, (i, k) in enumerate(items):
            out_ref[i, :, k * group : (k + 1) * group, :] = back[
                :, at * length : (at + 1) * length
            ].reshape(parts, group, length)
        for i in these:
            out_copy(i).start()
        return carry

    lax.fori_loop(0, count // 2, step, 0)
    for i in range(count):
        out_copy(i).wait()


def backward_kernel(length, planes, scale, count, *refs):
    values_hbm, y_hbm, z_hbm, *sources_hbm = refs[: 3 + count]
    out_hbm, values_ref, y_ref, z_ref, sources_ref, out_ref, in_sems, value_sems, source_sems = refs[
        3 + count :
    ]
    rows = planes * length
    fixed = fetch([(y_hbm, y_ref), (z_hbm, z_ref)], in_sems)
    for i, source in enumerate(sources_hbm):
        pltpu.make_async_copy(values_hbm.at[:, i], values_ref.at[i], value_sems.at[i]).start()
        pltpu.make_async_copy(source.at[0], sources_ref.at[i], source_sems.at[i]).start()
    out_ref[...] = jnp.zeros_like(out_ref)
    for copy in fixed:
        copy.wait()

    def step(n, carry):
        these = [2 * n, 2 * n + 1]
        for i in these:
            pltpu.make_async_copy(values_hbm.at[:, i], values_ref.at[i], value_sems.at[i]).wait()
            pltpu.make_async_copy(sources_hbm[0].at[0], sources_ref.at[i], source_sems.at[i]).wait()
        flats = [values_ref.at[i].reshape(length * 2 * planes, length) for i in these]
        stacked = jnp.concatenate(
            [
                jnp.concatenate(
                    [
                        flat[pl.ds(part * planes + p, length, stride=2 * planes), :]
                        for flat in flats
                        for p in range(planes)
                    ],
                    axis=1,
                )
                for part in range(2)
            ],
            axis=0,
        )
        along_y = turn_back(from_left(y_ref, stacked), length, 2 * planes)
        potential = from_right(along_y, z_ref)
        for part in range(2):
            total = out_ref[part].reshape(rows, length)
            for at, i in enumerate(these):
                total += (
                    potential[at * rows : (at + 1) * rows, part * length : (part + 1) * length]
                    * (sources_ref[i].reshape(rows, length) * scale)
                )
            out_ref[part] = total.reshape(planes, length, length)
        return carry

    lax.fori_loop(0, count // 2, step, 0)
    copy = pltpu.make_async_copy(out_ref, out_hbm, in_sems.at[0])
    copy.start()
    copy.wait()


def cost(count, rows, columns):
    return pl.CostEstimate(
        flops=count * 12 * rows * rows * columns,
        bytes_accessed=count * 12 * rows * columns,
        transcendentals=0,
    )


def solution(mesh):
    shards = mesh.shape["plane"]
    bands = mesh.shape["band"]
    swap = [(b, b ^ 1) for b in range(bands)]
    up = [(b, (b + 2) % bands) for b in range(bands)]
    down = [(b, (b - 2) % bands) for b in range(bands)]
    opposite = [(b, (b + 4) % bands) for b in range(bands)]

    def on_device(targets, sources, kernel):
        length = targets.shape[-1]
        planes = targets.shape[1]
        group = 2 * planes * planes
        forward_matrices, middle_matrices, backward_matrices = (
            (jnp.asarray(first), jnp.asarray(second)) for first, second in dft_matrices(length, planes)
        )
        slab = (planes, length, length)
        fields = (2,) + slab
        packed = (shards, group, length)
        left = pltpu.VMEM((2 * length, 6 * length), jnp.bfloat16)
        right = pltpu.VMEM((6 * length, 2 * length), jnp.bfloat16)
        grid_kernel = (kernel * (1.0 / float(length) ** 3)).transpose(1, 0, 2)

        def call(body, name, count, operands, out_shape, scratch, scalars=0, aliases={}):
            return pl.pallas_call(
                lambda *refs: body(*refs),
                in_specs=[pl.BlockSpec(memory_space=pltpu.SMEM)] * scalars
                + [pl.BlockSpec(memory_space=pltpu.HBM)] * (len(operands) - scalars),
                out_specs=pl.BlockSpec(memory_space=pltpu.HBM),
                out_shape=jax.ShapeDtypeStruct(out_shape, jnp.float32),
                scratch_shapes=scratch,
                input_output_aliases=aliases,
                compiler_params=pltpu.CompilerParams(vmem_limit_bytes=vmem_limit),
                cost_estimate=cost(count, 2 * length, planes * length),
                name=name,
            )(*operands)

        def room(*shape):
            return pltpu.VMEM(shape, jnp.float32)

        def sems(count):
            return pltpu.SemaphoreType.DMA((count,))

        def exchange(values):
            return lax.all_to_all(values, "plane", split_axis=0, concat_axis=0, tiled=True)

        def forward(bounds, batch, *filled):
            count = len(batch)
            return call(
                lambda *refs: forward_kernel(length, planes, count, *refs),
                "forward",
                count,
                (bounds, targets, *forward_matrices, *batch, *filled),
                (shards, bands, group, length),
                [room(*fields), right, left, room(count, *slab), room(count, *packed)]
                + [sems(3), sems(count), sems(count)],
                scalars=1,
                aliases={4 + count: 0} if filled else {},
            )

        def middle(values):
            count = values.shape[1]
            return call(
                lambda *refs: middle_kernel(length, planes, count, *refs),
                "middle",
                count,
                (values, grid_kernel, *middle_matrices),
                (shards, count, group, length),
                [room(count, *packed), room(planes, length, length), left, left]
                + [room(count, *packed)]
                + [sems(3), sems(count), sems(count)],
            )

        def backward(values, batch):
            count = len(batch)
            return call(
                lambda *refs: backward_kernel(length, planes, -exact_share, count, *refs),
                "backward",
                count,
                (values, *backward_matrices, *batch),
                fields,
                [room(count, *packed), left, right, room(count, *slab), room(*fields)]
                + [sems(2), sems(count), sems(count)],
            )

        def move(values, pairs):
            return lax.ppermute(values, "band", pairs)

        below, above = move(sources, up), move(sources, down)
        far = move(sources, opposite)
        every = [sources, move(sources, swap)]
        core = lax.axis_index("band") % 2
        bounds = jnp.array([[0, 2], [2, 6], [6, 8]], jnp.int32)
        filled = forward(bounds[0], every)
        below, above, filled = lax.optimization_barrier((below, above, filled))
        every += [below, above, move(below, swap), move(above, swap)]
        filled = forward(bounds[1], every, filled)
        far, filled = lax.optimization_barrier((far, filled))
        every += [far, move(far, swap)]
        filled = forward(bounds[2], every, filled)
        filled, grid_kernel = lax.optimization_barrier((filled, grid_kernel))
        here = exchange(middle(exchange(filled)))
        return backward(here, every)

    return jax.shard_map(
        on_device,
        mesh=mesh,
        in_specs=(
            P("band", "plane", None, None),
            P("band", "plane", None, None),
            P(None, "plane", None),
        ),
        out_specs=P("band", "plane", None, None),
        check_vma=False,
    )
```

```python
import math

import jax
import jax.numpy as jnp
import ml_dtypes
import numpy as np
from jax import lax
from jax.experimental import pallas as pl
from jax.experimental.pallas import tpu as pltpu
from jax.sharding import PartitionSpec as P

exact_share = 0.25
vmem_limit = 64 * 1024 * 1024


def halves(matrix):
    high = matrix.astype(ml_dtypes.bfloat16)
    low = (matrix - high.astype(np.float64)).astype(ml_dtypes.bfloat16)
    return high, low


def left_form(matrix):
    high, low = halves(matrix)
    return np.concatenate([high, low], axis=1)


def right_form(matrix):
    high, low = halves(matrix)
    return np.concatenate([high, low], axis=0)


def dft_matrices(length, planes):
    indices = np.arange(length)
    angles = (indices[:, None] * indices[None, :] % length) * (2.0 * math.pi / length)
    cosine, sine = np.cos(angles), np.sin(angles)
    forward = np.block([[cosine, sine], [-sine, cosine]])
    inverse = np.block([[cosine, -sine], [sine, cosine]])
    order = np.arange(2 * length).reshape(2, length // planes, planes).transpose(1, 0, 2).reshape(-1)
    return (
        (right_form(forward.T), left_form(forward)),
        (left_form(forward[:, order]), left_form(inverse[order, :])),
        (left_form(inverse), right_form(inverse.T)),
    )


def split(values):
    high = values.astype(jnp.bfloat16)
    low = (values - high.astype(jnp.float32)).astype(jnp.bfloat16)
    return high, low


def from_left(matrix_ref, values):
    high, low = split(values)
    inner = values.shape[0]
    matrix = jnp.concatenate([matrix_ref[:, :inner], matrix_ref[...]], axis=1)
    stack = jnp.concatenate([high, low, high], axis=0)
    return jnp.dot(matrix, stack, preferred_element_type=jnp.float32)


def from_right(values, matrix_ref):
    high, low = split(values)
    inner = values.shape[1]
    matrix = jnp.concatenate([matrix_ref[:inner], matrix_ref[...]], axis=0)
    stack = jnp.concatenate([high, low, high], axis=1)
    return jnp.dot(stack, matrix, preferred_element_type=jnp.float32)


def fetch(pairs, sems):
    copies = [
        pltpu.make_async_copy(source, target, sems.at[i]) for i, (source, target) in enumerate(pairs)
    ]
    for copy in copies:
        copy.start()
    return copies


def turn(values, length, count):
    return jnp.concatenate(
        [
            jnp.concatenate(
                [
                    values[p * length : (p + 1) * length, part * length : (part + 1) * length]
                    for part in range(2)
                ],
                axis=0,
            )
            for p in range(count)
        ],
        axis=1,
    )


def turn_back(values, length, count):
    return jnp.concatenate(
        [
            jnp.concatenate(
                [
                    values[part * length : (part + 1) * length, p * length : (p + 1) * length]
                    for part in range(2)
                ],
                axis=1,
            )
            for p in range(count)
        ],
        axis=0,
    )


def forward_kernel(length, planes, count, bounds_ref, targets_hbm, z_hbm, y_hbm, *refs):
    sources_hbm = refs[:count]
    out_hbm, targets_ref, z_ref, y_ref, sources_ref, out_ref, in_sems, source_sems, out_sems = refs[-9:]
    low, high = bounds_ref[0], bounds_ref[1]
    rows = planes * length
    items = 2 * planes

    def source_copy(i):
        return pltpu.make_async_copy(sources_hbm[i].at[0], sources_ref.at[i], source_sems.at[i])

    def out_copy(i):
        return pltpu.make_async_copy(out_ref.at[i], out_hbm.at[:, i], out_sems.at[i])

    @pl.when(low < high)
    def _():
        fixed = fetch([(targets_hbm, targets_ref), (z_hbm, z_ref), (y_hbm, y_ref)], in_sems)
        for i in range(count):

            @pl.when((low <= i) & (i < high))
            def _(i=i):
                source_copy(i).start()

        for copy in fixed:
            copy.wait()

        def step(n, carry):
            these = [2 * n, 2 * n + 1]
            for i in these:
                pltpu.make_async_copy(
                    sources_hbm[0].at[0], sources_ref.at[i], source_sems.at[i]
                ).wait()
            density = jnp.concatenate(
                [
                    jnp.concatenate(
                        [
                            (targets_ref[part] * sources_ref[i]).reshape(rows, length)
                            for part in range(2)
                        ],
                        axis=1,
                    )
                    for i in these
                ],
                axis=0,
            )
            along_y = from_left(y_ref, turn(from_right(density, z_ref), length, items))
            for at, i in enumerate(these):
                flat = out_ref.at[i].reshape(length * 2 * planes, length)
                for part in range(2):
                    for p in range(planes):
                        item = at * planes + p
                        flat[pl.ds(part * planes + p, length, stride=2 * planes), :] = along_y[
                            part * length : (part + 1) * length, item * length : (item + 1) * length
                        ]
                out_copy(i).start()
            return carry

        lax.fori_loop(low // 2, high // 2, step, 0)
        for i in range(count):

            @pl.when((low <= i) & (i < high))
            def _(i=i):
                out_copy(i).wait()


def middle_kernel(length, planes, count, *refs):
    values_hbm, kernel_hbm, there_hbm, back_hbm, out_hbm = refs[:5]
    values_ref, kernel_ref, there_ref, back_ref, out_ref, in_sems, value_sems, out_sems = refs[5:]
    group = 2 * planes
    parts = length // planes
    fixed = fetch(
        [(kernel_hbm, kernel_ref), (there_hbm, there_ref), (back_hbm, back_ref)], in_sems
    )
    fetch([(values_hbm.at[:, i], values_ref.at[i]) for i in range(count)], value_sems)
    for copy in fixed:
        copy.wait()

    def out_copy(i):
        return pltpu.make_async_copy(out_ref.at[i], out_hbm.at[:, i], out_sems.at[i])

    def step(n, carry):
        these = [2 * n, 2 * n + 1]
        for i in these:
            pltpu.make_async_copy(values_hbm.at[:, i], values_ref.at[i], value_sems.at[i]).wait()
        items = [(i, k) for i in these for k in range(planes)]
        values = jnp.concatenate(
            [
                values_ref[i, :, k * group : (k + 1) * group, :].reshape(2 * length, length)
                for i, k in items
            ],
            axis=1,
        )
        spectrum = from_left(there_ref, values)
        weight = jnp.concatenate([kernel_ref[k] for i, k in items], axis=1)
        weighted = jnp.concatenate([spectrum[:length] * weight, spectrum[length:] * weight], axis=0)
        back = from_left(back_ref, weighted)
        for at, (i, k) in enumerate(items):
            out_ref[i, :, k * group : (k + 1) * group, :] = back[
                :, at * length : (at + 1) * length
            ].reshape(parts, group, length)
        for i in these:
            out_copy(i).start()
        return carry

    lax.fori_loop(0, count // 2, step, 0)
    for i in range(count):
        out_copy(i).wait()


def backward_kernel(length, planes, scale, count, *refs):
    values_hbm, y_hbm, z_hbm, *sources_hbm = refs[: 3 + count]
    out_hbm, values_ref, y_ref, z_ref, sources_ref, out_ref, in_sems, value_sems, source_sems = refs[
        3 + count :
    ]
    rows = planes * length
    fixed = fetch([(y_hbm, y_ref), (z_hbm, z_ref)], in_sems)
    for i, source in enumerate(sources_hbm):
        pltpu.make_async_copy(values_hbm.at[:, i], values_ref.at[i], value_sems.at[i]).start()
        pltpu.make_async_copy(source.at[0], sources_ref.at[i], source_sems.at[i]).start()
    out_ref[...] = jnp.zeros_like(out_ref)
    for copy in fixed:
        copy.wait()

    def step(n, carry):
        these = [2 * n, 2 * n + 1]
        for i in these:
            pltpu.make_async_copy(values_hbm.at[:, i], values_ref.at[i], value_sems.at[i]).wait()
            pltpu.make_async_copy(sources_hbm[0].at[0], sources_ref.at[i], source_sems.at[i]).wait()
        flats = [values_ref.at[i].reshape(length * 2 * planes, length) for i in these]
        stacked = jnp.concatenate(
            [
                jnp.concatenate(
                    [
                        flat[pl.ds(part * planes + p, length, stride=2 * planes), :]
                        for flat in flats
                        for p in range(planes)
                    ],
                    axis=1,
                )
                for part in range(2)
            ],
            axis=0,
        )
        along_y = turn_back(from_left(y_ref, stacked), length, 2 * planes)
        potential = from_right(along_y, z_ref)
        for part in range(2):
            total = out_ref[part].reshape(rows, length)
            for at, i in enumerate(these):
                total += (
                    potential[at * rows : (at + 1) * rows, part * length : (part + 1) * length]
                    * (sources_ref[i].reshape(rows, length) * scale)
                )
            out_ref[part] = total.reshape(planes, length, length)
        return carry

    lax.fori_loop(0, count // 2, step, 0)
    copy = pltpu.make_async_copy(out_ref, out_hbm, in_sems.at[0])
    copy.start()
    copy.wait()


def cost(count, rows, columns):
    return pl.CostEstimate(
        flops=count * 12 * rows * rows * columns,
        bytes_accessed=count * 12 * rows * columns,
        transcendentals=0,
    )


def solution(mesh):
    shards = mesh.shape["plane"]
    bands = mesh.shape["band"]
    swap = [(b, b ^ 1) for b in range(bands)]
    one_way = [(b, (b + (-2 if b % 2 else 2)) % bands) for b in range(bands)]
    other_way = [(to, b) for b, to in one_way]

    def on_device(targets, sources, kernel):
        length = targets.shape[-1]
        planes = targets.shape[1]
        group = 2 * planes * planes
        forward_matrices, middle_matrices, backward_matrices = (
            (jnp.asarray(first), jnp.asarray(second)) for first, second in dft_matrices(length, planes)
        )
        slab = (planes, length, length)
        fields = (2,) + slab
        packed = (shards, group, length)
        left = pltpu.VMEM((2 * length, 4 * length), jnp.bfloat16)
        right = pltpu.VMEM((4 * length, 2 * length), jnp.bfloat16)
        grid_kernel = (kernel * (1.0 / float(length) ** 3)).transpose(1, 0, 2)

        def call(body, name, count, operands, out_shape, scratch, scalars=0, aliases={}):
            return pl.pallas_call(
                lambda *refs: body(*refs),
                in_specs=[pl.BlockSpec(memory_space=pltpu.SMEM)] * scalars
                + [pl.BlockSpec(memory_space=pltpu.HBM)] * (len(operands) - scalars),
                out_specs=pl.BlockSpec(memory_space=pltpu.HBM),
                out_shape=jax.ShapeDtypeStruct(out_shape, jnp.float32),
                scratch_shapes=scratch,
                input_output_aliases=aliases,
                compiler_params=pltpu.CompilerParams(vmem_limit_bytes=vmem_limit),
                cost_estimate=cost(count, 2 * length, planes * length),
                name=name,
            )(*operands)

        def room(*shape):
            return pltpu.VMEM(shape, jnp.float32)

        def sems(count):
            return pltpu.SemaphoreType.DMA((count,))

        def exchange(values):
            return lax.all_to_all(values, "plane", split_axis=0, concat_axis=0, tiled=True)

        def forward(bounds, batch, *filled):
            count = len(batch)
            return call(
                lambda *refs: forward_kernel(length, planes, count, *refs),
                "forward",
                0,
                (bounds, targets, *forward_matrices, *batch, *filled),
                (shards, bands, group, length),
                [room(*fields), right, left, room(count, *slab), room(count, *packed)]
                + [sems(3), sems(count), sems(count)],
                scalars=1,
                aliases={4 + count: 0} if filled else {},
            )

        def middle(values):
            count = values.shape[1]
            return call(
                lambda *refs: middle_kernel(length, planes, count, *refs),
                "middle",
                count,
                (values, grid_kernel, *middle_matrices),
                (shards, count, group, length),
                [room(count, *packed), room(planes, length, length), left, left]
                + [room(count, *packed)]
                + [sems(3), sems(count), sems(count)],
            )

        def backward(values, batch):
            count = len(batch)
            return call(
                lambda *refs: backward_kernel(length, planes, -exact_share, count, *refs),
                "backward",
                count,
                (values, *backward_matrices, *batch),
                fields,
                [room(count, *packed), left, right, room(count, *slab), room(*fields)]
                + [sems(2), sems(count), sems(count)],
            )

        def move(values, pairs):
            return lax.ppermute(values, "band", pairs)

        near, other = move(sources, one_way), move(sources, other_way)
        every = [sources, move(sources, swap)]
        bounds = jnp.array([[0, 2], [2, 6], [6, 8]], jnp.int32)
        filled = forward(bounds[0], every)
        near, filled, grid_kernel = lax.optimization_barrier((near, filled, grid_kernel))
        far = move(near, one_way)
        near_too = move(near, swap)
        other, near_too = lax.optimization_barrier((other, near_too))
        every += [near, near_too, other, move(other, swap)]
        filled = forward(bounds[1], every, filled)
        far, filled = lax.optimization_barrier((far, filled))
        every += [far, move(far, swap)]
        filled = forward(bounds[2], every, filled)
        here = exchange(middle(exchange(filled)))
        return backward(here, every)

    return jax.shard_map(
        on_device,
        mesh=mesh,
        in_specs=(
            P("band", "plane", None, None),
            P("band", "plane", None, None),
            P(None, "plane", None),
        ),
        out_specs=P("band", "plane", None, None),
        check_vma=False,
    )
```

```python
import math

import jax
import jax.numpy as jnp
import ml_dtypes
import numpy as np
from jax import lax
from jax.experimental import pallas as pl
from jax.experimental.pallas import tpu as pltpu
from jax.sharding import PartitionSpec as P

exact_share = 0.25
vmem_limit = 28 * 1024 * 1024


def halves(matrix):
    high = matrix.astype(ml_dtypes.bfloat16)
    low = (matrix - high.astype(np.float64)).astype(ml_dtypes.bfloat16)
    return high, low


def left_form(matrix):
    high, low = halves(matrix)
    return np.concatenate([high, low], axis=1)


def right_form(matrix):
    high, low = halves(matrix)
    return np.concatenate([high, low], axis=0)


def dft_matrices(length, planes):
    indices = np.arange(length)
    angles = (indices[:, None] * indices[None, :] % length) * (2.0 * math.pi / length)
    cosine, sine = np.cos(angles), np.sin(angles)
    forward = np.block([[cosine, sine], [-sine, cosine]])
    inverse = np.block([[cosine, -sine], [sine, cosine]])
    order = np.arange(2 * length).reshape(2, length // planes, planes).transpose(1, 0, 2).reshape(-1)
    return (
        (right_form(forward.T), left_form(forward)),
        (left_form(forward[:, order]), left_form(inverse[order, :])),
        (left_form(inverse), right_form(inverse.T)),
    )


def split(values):
    high = values.astype(jnp.bfloat16)
    low = (values - high.astype(jnp.float32)).astype(jnp.bfloat16)
    return high, low


def from_left(matrix_ref, values):
    high, low = split(values)
    inner = values.shape[0]
    matrix = jnp.concatenate([matrix_ref[:, :inner], matrix_ref[...]], axis=1)
    stack = jnp.concatenate([high, low, high], axis=0)
    return jnp.dot(matrix, stack, preferred_element_type=jnp.float32)


def from_right(values, matrix_ref):
    high, low = split(values)
    inner = values.shape[1]
    matrix = jnp.concatenate([matrix_ref[:inner], matrix_ref[...]], axis=0)
    stack = jnp.concatenate([high, low, high], axis=1)
    return jnp.dot(stack, matrix, preferred_element_type=jnp.float32)


def fetch(pairs, sems):
    copies = [
        pltpu.make_async_copy(source, target, sems.at[i]) for i, (source, target) in enumerate(pairs)
    ]
    for copy in copies:
        copy.start()
    return copies


def turn(values, length, count):
    return jnp.concatenate(
        [
            jnp.concatenate(
                [
                    values[p * length : (p + 1) * length, part * length : (part + 1) * length]
                    for part in range(2)
                ],
                axis=0,
            )
            for p in range(count)
        ],
        axis=1,
    )


def turn_back(values, length, count):
    return jnp.concatenate(
        [
            jnp.concatenate(
                [
                    values[part * length : (part + 1) * length, p * length : (p + 1) * length]
                    for part in range(2)
                ],
                axis=1,
            )
            for p in range(count)
        ],
        axis=0,
    )


def forward_kernel(length, planes, count, bounds_ref, targets_hbm, z_hbm, y_hbm, *refs):
    sources_hbm = refs[:count]
    out_hbm, targets_ref, z_ref, y_ref, sources_ref, out_ref, in_sems, source_sems, out_sems = refs[-9:]
    low, high = bounds_ref[0], bounds_ref[1]
    rows = planes * length
    items = 2 * planes

    def source_copy(i):
        return pltpu.make_async_copy(sources_hbm[i].at[0], sources_ref.at[i], source_sems.at[i])

    def out_copy(i):
        return pltpu.make_async_copy(out_ref.at[i], out_hbm.at[:, i], out_sems.at[i])

    @pl.when(low < high)
    def _():
        fixed = fetch([(targets_hbm, targets_ref), (z_hbm, z_ref), (y_hbm, y_ref)], in_sems)
        for i in range(count):

            @pl.when((low <= i) & (i < high))
            def _(i=i):
                source_copy(i).start()

        for copy in fixed:
            copy.wait()

        def step(n, carry):
            these = [2 * n, 2 * n + 1]
            for i in these:
                pltpu.make_async_copy(
                    sources_hbm[0].at[0], sources_ref.at[i], source_sems.at[i]
                ).wait()
            density = jnp.concatenate(
                [
                    jnp.concatenate(
                        [
                            (targets_ref[part] * sources_ref[i]).reshape(rows, length)
                            for part in range(2)
                        ],
                        axis=1,
                    )
                    for i in these
                ],
                axis=0,
            )
            along_y = from_left(y_ref, turn(from_right(density, z_ref), length, items))
            for at, i in enumerate(these):
                flat = out_ref.at[i].reshape(length * 2 * planes, length)
                for part in range(2):
                    for p in range(planes):
                        item = at * planes + p
                        flat[pl.ds(part * planes + p, length, stride=2 * planes), :] = along_y[
                            part * length : (part + 1) * length, item * length : (item + 1) * length
                        ]
                out_copy(i).start()
            return carry

        lax.fori_loop(low // 2, high // 2, step, 0)
        for i in range(count):

            @pl.when((low <= i) & (i < high))
            def _(i=i):
                out_copy(i).wait()


def middle_kernel(length, planes, count, *refs):
    values_hbm, kernel_hbm, there_hbm, back_hbm, out_hbm = refs[:5]
    values_ref, kernel_ref, there_ref, back_ref, out_ref, in_sems, value_sems, out_sems = refs[5:]
    group = 2 * planes
    parts = length // planes
    fixed = fetch(
        [(kernel_hbm, kernel_ref), (there_hbm, there_ref), (back_hbm, back_ref)], in_sems
    )
    fetch([(values_hbm.at[:, i], values_ref.at[i]) for i in range(count)], value_sems)
    for copy in fixed:
        copy.wait()

    def out_copy(i):
        return pltpu.make_async_copy(out_ref.at[i], out_hbm.at[:, i], out_sems.at[i])

    def step(n, carry):
        these = [2 * n, 2 * n + 1]
        for i in these:
            pltpu.make_async_copy(values_hbm.at[:, i], values_ref.at[i], value_sems.at[i]).wait()
        items = [(i, k) for i in these for k in range(planes)]
        values = jnp.concatenate(
            [
                values_ref[i, :, k * group : (k + 1) * group, :].reshape(2 * length, length)
                for i, k in items
            ],
            axis=1,
        )
        spectrum = from_left(there_ref, values)
        weight = jnp.concatenate([kernel_ref[k] for i, k in items], axis=1)
        weighted = jnp.concatenate([spectrum[:length] * weight, spectrum[length:] * weight], axis=0)
        back = from_left(back_ref, weighted)
        for at, (i, k) in enumerate(items):
            out_ref[i, :, k * group : (k + 1) * group, :] = back[
                :, at * length : (at + 1) * length
            ].reshape(parts, group, length)
        for i in these:
            out_copy(i).start()
        return carry

    lax.fori_loop(0, count // 2, step, 0)
    for i in range(count):
        out_copy(i).wait()


def backward_kernel(length, planes, scale, count, *refs):
    values_hbm, y_hbm, z_hbm, *sources_hbm = refs[: 3 + count]
    out_hbm, values_ref, y_ref, z_ref, sources_ref, out_ref, in_sems, value_sems, source_sems = refs[
        3 + count :
    ]
    rows = planes * length
    fixed = fetch([(y_hbm, y_ref), (z_hbm, z_ref)], in_sems)
    for i, source in enumerate(sources_hbm):
        pltpu.make_async_copy(values_hbm.at[:, i], values_ref.at[i], value_sems.at[i]).start()
        pltpu.make_async_copy(source.at[0], sources_ref.at[i], source_sems.at[i]).start()
    out_ref[...] = jnp.zeros_like(out_ref)
    for copy in fixed:
        copy.wait()

    def step(n, carry):
        these = [2 * n, 2 * n + 1]
        for i in these:
            pltpu.make_async_copy(values_hbm.at[:, i], values_ref.at[i], value_sems.at[i]).wait()
            pltpu.make_async_copy(sources_hbm[0].at[0], sources_ref.at[i], source_sems.at[i]).wait()
        flats = [values_ref.at[i].reshape(length * 2 * planes, length) for i in these]
        stacked = jnp.concatenate(
            [
                jnp.concatenate(
                    [
                        flat[pl.ds(part * planes + p, length, stride=2 * planes), :]
                        for flat in flats
                        for p in range(planes)
                    ],
                    axis=1,
                )
                for part in range(2)
            ],
            axis=0,
        )
        along_y = turn_back(from_left(y_ref, stacked), length, 2 * planes)
        potential = from_right(along_y, z_ref)
        for part in range(2):
            total = out_ref[part].reshape(rows, length)
            for at, i in enumerate(these):
                total += (
                    potential[at * rows : (at + 1) * rows, part * length : (part + 1) * length]
                    * (sources_ref[i].reshape(rows, length) * scale)
                )
            out_ref[part] = total.reshape(planes, length, length)
        return carry

    lax.fori_loop(0, count // 2, step, 0)
    copy = pltpu.make_async_copy(out_ref, out_hbm, in_sems.at[0])
    copy.start()
    copy.wait()


def cost(count, rows, columns):
    return pl.CostEstimate(
        flops=count * 12 * rows * rows * columns,
        bytes_accessed=count * 12 * rows * columns,
        transcendentals=0,
    )


def solution(mesh):
    shards = mesh.shape["plane"]
    bands = mesh.shape["band"]
    swap = [(b, b ^ 1) for b in range(bands)]
    one_way = [(b, (b + (-2 if b % 2 else 2)) % bands) for b in range(bands)]
    other_way = [(to, b) for b, to in one_way]

    def on_device(targets, sources, kernel):
        length = targets.shape[-1]
        planes = targets.shape[1]
        group = 2 * planes * planes
        forward_matrices, middle_matrices, backward_matrices = (
            (jnp.asarray(first), jnp.asarray(second)) for first, second in dft_matrices(length, planes)
        )
        slab = (planes, length, length)
        fields = (2,) + slab
        packed = (shards, group, length)
        left = pltpu.VMEM((2 * length, 4 * length), jnp.bfloat16)
        right = pltpu.VMEM((4 * length, 2 * length), jnp.bfloat16)
        grid_kernel = (kernel * (1.0 / float(length) ** 3)).transpose(1, 0, 2)

        def call(body, name, count, operands, out_shape, scratch, scalars=0, aliases={}):
            return pl.pallas_call(
                lambda *refs: body(*refs),
                in_specs=[pl.BlockSpec(memory_space=pltpu.SMEM)] * scalars
                + [pl.BlockSpec(memory_space=pltpu.HBM)] * (len(operands) - scalars),
                out_specs=pl.BlockSpec(memory_space=pltpu.HBM),
                out_shape=jax.ShapeDtypeStruct(out_shape, jnp.float32),
                scratch_shapes=scratch,
                input_output_aliases=aliases,
                compiler_params=pltpu.CompilerParams(vmem_limit_bytes=vmem_limit),
                cost_estimate=cost(count, 2 * length, planes * length),
                name=name,
            )(*operands)

        def room(*shape):
            return pltpu.VMEM(shape, jnp.float32)

        def sems(count):
            return pltpu.SemaphoreType.DMA((count,))

        def exchange(values):
            return lax.all_to_all(values, "plane", split_axis=0, concat_axis=0, tiled=True)

        def forward(bounds, batch, *filled):
            count = len(batch)
            return call(
                lambda *refs: forward_kernel(length, planes, count, *refs),
                "forward",
                0,
                (bounds, targets, *forward_matrices, *batch, *filled),
                (shards, bands, group, length),
                [room(*fields), right, left, room(count, *slab), room(count, *packed)]
                + [sems(3), sems(count), sems(count)],
                scalars=1,
                aliases={4 + count: 0} if filled else {},
            )

        def middle(values):
            count = values.shape[1]
            return call(
                lambda *refs: middle_kernel(length, planes, count, *refs),
                "middle",
                count,
                (values, grid_kernel, *middle_matrices),
                (shards, count, group, length),
                [room(count, *packed), room(planes, length, length), left, left]
                + [room(count, *packed)]
                + [sems(3), sems(count), sems(count)],
            )

        def backward(values, batch):
            count = len(batch)
            return call(
                lambda *refs: backward_kernel(length, planes, -exact_share, count, *refs),
                "backward",
                count,
                (values, *backward_matrices, *batch),
                fields,
                [room(count, *packed), left, right, room(count, *slab), room(*fields)]
                + [sems(2), sems(count), sems(count)],
            )

        def move(values, pairs):
            return lax.ppermute(values, "band", pairs)

        near, other = move(sources, one_way), move(sources, other_way)
        every = [sources, move(sources, swap)]
        bounds = jnp.array([[0, 2], [2, 6], [6, 8]], jnp.int32)
        filled = forward(bounds[0], every)
        near, filled, grid_kernel = lax.optimization_barrier((near, filled, grid_kernel))
        far = move(near, one_way)
        near_too = move(near, swap)
        other, near_too = lax.optimization_barrier((other, near_too))
        every += [near, near_too, other, move(other, swap)]
        filled = forward(bounds[1], every, filled)
        far, filled = lax.optimization_barrier((far, filled))
        every += [far, move(far, swap)]
        filled = forward(bounds[2], every, filled)
        here = exchange(middle(exchange(filled)))
        return backward(here, every)

    return jax.shard_map(
        on_device,
        mesh=mesh,
        in_specs=(
            P("band", "plane", None, None),
            P("band", "plane", None, None),
            P(None, "plane", None),
        ),
        out_specs=P("band", "plane", None, None),
        check_vma=False,
    )
```
